128 devices in a mesh: field: 4 (over y_hi, core), space: 32 (over y_lo, x, z).
Axes of the slice: x: 4, y: 4 (y_hi: 2, y_lo: 2; y = y_hi * 2 + y_lo), z: 4, core: 2. Of those that a mesh axis runs over, the one named last changes fastest.
Arguments:
- fields: float32 [8, 22, 128, 32, 256], P('field', None, 'space'), may hold values from -6 to 6
- velocity: float32 [3, 128, 32, 256], P(None, 'space'), may hold values from -1 to 1
- noise: int32 [2, 2, 8, 3, 128, 32, 256], P(None, None, 'field', None, 'space'), may hold values from -1 to 1
- mixing_rate: float32 [128, 32, 256], P('space'), may hold values from 0.5 to 2
- parcel_cell: int32 [4, 32768], P('field', 'space'), may hold values from 0 to 32767
- parcel_mass: float32 [4, 32768], P('field', 'space'), may hold values from 0.5 to 2
- parcel_temp: float32 [4, 32768], P('field', 'space'), may hold values from 0.5 to 1.5
Outputs:
- new_fields: float32 [8, 22, 128, 32, 256], P('field', None, 'space')
- new_mass: float32 [4, 32768], P('field', 'space')
- new_temp: float32 [4, 32768], P('field', 'space')
The draws below stay inside these ranges and needn't reach their ends.
Inputs may be any that keep to these rules, and one draw needn't show every extreme that they name: parcel_cell is the parcel's cell within its block of 4 x 32 x 256 cells, ((x - first plane of the block) * 32 + y) * 256 + z; parcels of group g and block b stand in row g, columns b * 1024 to (b + 1) * 1024 - 1. `noise`: wiener increments in units of the substep's scale.
All inputs are finite; a program needn't handle non-finite values.
Results may differ from the reference program's by a relative error of at most 0.0001.
Values sent between devices are 32-bit elements; how exact they have to be, the bound alone decides.
A program may use at most 192 MiB of HBM per device.

```python
import math
import jax
import jax.numpy as jnp
from jax import lax

S = 22
CX = 4
NY = 32
NZ = 256
P_DEV = 1024
STEPS = 2
FIELDS = 8
GROUPS = 4
NX = 128
CELLS_DEV = 32768
PSPAN = 32768


def set_ends(array, rng, least, largest):
    index_at = [jax.random.randint(jax.random.fold_in(rng, axis), (), 0, length) for axis, length in enumerate(array.shape)]
    main_axis = array.shape.index(max(array.shape))
    next_to = index_at[:main_axis] + [(index_at[main_axis] + 1) % array.shape[main_axis]] + index_at[main_axis + 1:]
    return array.at[tuple(index_at)].set(least).at[tuple(next_to)].set(largest)


def block_levels(key, shape, shards, smallest, top_value):
    level = 1.0
    for position, shards_of in shards:
        draws = jax.random.uniform(jax.random.fold_in(jax.random.fold_in(key, 6), position), (shards_of,), jnp.float32, smallest / len(shards), top_value / len(shards))
        level = level * jnp.repeat(jnp.exp(draws), shape[position] // shards_of).reshape((-1,) + (1,) * (len(shape) - 1 - position))
    return level


def scatter_about(rng, shape, scale, bound, split=(), held_as=jnp.bfloat16):
    entries = scale * jax.random.normal(rng, shape, jnp.float32)
    if split:
        entries = entries * block_levels(rng, shape, split, -0.22, 0.18)
    return jnp.clip(entries, -bound, bound).astype(held_as)


def setup_inputs(seed: int = 0) -> dict:
    key_of = jax.random.split(jax.random.key(seed), 8)
    return {
        "fields": scatter_about(key_of[0], (FIELDS, S, NX, NY, NZ), 1.0, 6.0, ((0, 4), (2, 32)), jnp.float32),
        "velocity": jnp.clip(jax.random.uniform(key_of[1], (3, NX, NY, NZ), jnp.float32, -1.0, 1.0) * block_levels(key_of[1], (3, NX, NY, NZ), ((1, 32),), -0.4, 0.0), -1.0, 1.0),
        "noise": set_ends(jax.random.randint(key_of[2], (STEPS, 2, FIELDS, 3, NX, NY, NZ), -1, 2), jax.random.fold_in(key_of[2], 1), -1, 1).astype(jnp.int32),
        "mixing_rate": jnp.clip(jnp.exp(math.log(2.0) - 1.3862944 * jax.random.uniform(key_of[3], (NX, NY, NZ), jnp.float32) ** block_levels(key_of[3], (NX, NY, NZ), ((0, 32),), -0.2, 0.2)), 0.5, 2.0),
        "parcel_cell": set_ends(jax.random.randint(key_of[4], (GROUPS, PSPAN), 0, CX * NY * NZ), jax.random.fold_in(key_of[4], 1), 0, (CX * NY * NZ) - 1).astype(jnp.int32),
        "parcel_mass": jnp.clip(jnp.exp(math.log(2.0) - 1.3862944 * jax.random.uniform(key_of[5], (GROUPS, PSPAN), jnp.float32) ** block_levels(key_of[5], (GROUPS, PSPAN), ((0, 4), (1, 32)), -0.2, 0.2)), 0.5, 2.0),
        "parcel_temp": jnp.clip(0.5 + 1.0 * jax.random.uniform(key_of[6], (GROUPS, PSPAN), jnp.float32) ** block_levels(key_of[6], (GROUPS, PSPAN), ((0, 4), (1, 32)), -0.2, 0.2), 0.5, 1.5),
    }


sub_time = 0.2
diffusivity = 0.1
noise_gain = 0.2
step_time = 0.4
latent_heat = 0.5


def advance(padded, velocity, noise_now):
    center = padded[:, :, 1:-1]
    neighbours = [(padded[:, :, :-2], padded[:, :, 2:]),
                  (jnp.roll(center, 1, 3), jnp.roll(center, -1, 3)),
                  (jnp.roll(center, 1, 4), jnp.roll(center, -1, 4))]
    advect = jnp.zeros_like(center)
    spread = -6.0 * center
    stirred = jnp.zeros_like(center)
    for direction in range(3):
        lower_side, upper_side = neighbours[direction]
        speed_now = velocity[direction][None, None]
        advect = advect + jnp.maximum(speed_now, 0.0) * (center - lower_side) + jnp.minimum(speed_now, 0.0) * (upper_side - center)
        spread = spread + lower_side + upper_side
        stirred = stirred + 0.5 * (upper_side - lower_side) * noise_now[:, direction][:, None].astype(jnp.float32)
    return center + sub_time * (diffusivity * spread - advect) + noise_gain * stirred


def evaporate(mass, temper, vapor, gas_heat):
    sat_frac = 0.8 * jax.nn.sigmoid(4.0 * (temper - 1.0))
    drive = jnp.maximum(sat_frac - vapor, 0.0) / (1.0 - sat_frac)
    rate_now = mass * jnp.log1p(drive)
    heat_now = rate_now * (gas_heat - latent_heat)
    return rate_now, heat_now, mass - step_time * rate_now, temper + step_time * (gas_heat - temper)


def relax(moved, mean_field, mixing_rate, sources):
    mixed = moved - step_time * mixing_rate * (moved - mean_field)
    return mixed.at[:, 0:2].add(step_time * sources[None])


def reference(fields, velocity, noise, mixing_rate, parcel_cell, parcel_mass, parcel_temp):
    block_of = (jnp.arange(PSPAN) // P_DEV).astype(jnp.int32)
    global_cell = (block_of * CELLS_DEV)[None, :] + parcel_cell
    flat_cell = global_cell.reshape(-1)
    for step in range(STEPS):
        for sub_step in range(2):
            padded = jnp.concatenate([fields[:, :, -1:], fields, fields[:, :, :1]], axis=2)
            fields = lax.map(lambda pair_in: advance(pair_in[0][None], velocity, pair_in[1][None])[0],
                             (padded, noise[step, sub_step]))
        mean_field = jnp.sum(fields, axis=0) / FIELDS
        vapor = mean_field[0].reshape(-1)[global_cell]
        gas_heat = mean_field[1].reshape(-1)[global_cell]
        rate_now, heat_now, parcel_mass, parcel_temp = evaporate(parcel_mass, parcel_temp, vapor, gas_heat)
        total = NX * NY * NZ
        sources = jnp.stack([jax.ops.segment_sum(rate_now.reshape(-1), flat_cell, num_segments=total),
                             jax.ops.segment_sum(heat_now.reshape(-1), flat_cell, num_segments=total)]).reshape(2, NX, NY, NZ)
        fields = relax(fields, mean_field, mixing_rate, sources)
    return fields, parcel_mass, parcel_temp
```

```python
import jax
import jax.numpy as jnp
from jax import lax
from jax.experimental import pallas as pl
from jax.experimental.pallas import tpu as pltpu
from jax.sharding import PartitionSpec as P

MESH = pl.DeviceIdType.MESH
F32 = jnp.float32
BF16 = jnp.bfloat16

S, CX, NY, NZ = 22, 4, 32, 256
CHUNKS = S // 2
GROUPS, P_DEV = 4, 1024
ROWS = CX * NY
P_BLOCK = 512

sub_time = 0.2
diffusivity = 0.1
noise_gain = 0.2
step_time = 0.4
latent_heat = 0.5

LAG_TOTAL = 3
LAG_RELAX = 4


def split3(value):
    top = value.astype(BF16)
    rest = value - top.astype(F32)
    middle = rest.astype(BF16)
    return top, middle, (rest - middle.astype(F32)).astype(BF16)


def kernel(
    fields_in, velocity_in, noise_in, mixing_in, cell_in, mass_in, temp_in,
    fields_out, mass_out, temp_out,
    old, new, halo, noise, velocity, weight, coef, coef_mid,
    part, part_land, pair, pair_land, mean, source,
    cells, masses, temps,
    load_sem, parcel_load_sem, halo_send, halo_recv, mean_send, mean_recv,
    parcel_send, parcel_recv, out_sem,
):
    f = lax.axis_index("field")
    s = lax.axis_index("space")
    blocks = lax.axis_size("space")
    core = lax.rem(f, 2)
    above = {"space": lax.rem(s + 1, blocks)}
    below = {"space": lax.rem(s + blocks - 1, blocks)}
    twin = {"field": f + 1 - 2 * core}
    across = {"field": lax.rem(f + 2, 4)}
    corner = {"field": 3 - f}

    loads = [
        pltpu.make_async_copy(velocity_in, velocity, load_sem.at[0]),
        pltpu.make_async_copy(noise_in, noise, load_sem.at[1]),
        pltpu.make_async_copy(fields_in, old, load_sem.at[2]),
        pltpu.make_async_copy(mixing_in, weight, load_sem.at[3]),
    ]
    for load in loads:
        load.start()
    parcel_loads = [
        pltpu.make_async_copy(array, held.at[f], parcel_load_sem.at[k])
        for k, (array, held) in enumerate(((cell_in, cells), (mass_in, masses), (temp_in, temps)))
    ]
    for load in parcel_loads:
        load.start()

    barrier = pltpu.get_barrier_semaphore()
    for peer in (above, below, twin, across, corner):
        pl.semaphore_signal(barrier, 1, device_id=peer, device_id_type=MESH)
    pl.semaphore_wait(barrier, 5)

    def halo_copy(phase, side, c):
        plane = CX - 1 if side == 0 else 0
        held = (fields_in, new, old, new)[phase]
        return pltpu.make_async_remote_copy(
            src_ref=held.at[:, pl.ds(2 * c, 2), plane],
            dst_ref=halo.at[phase, side, :, pl.ds(2 * c, 2)],
            send_sem=halo_send.at[phase, side, c],
            recv_sem=halo_recv.at[phase, side, c],
            device_id=above if side == 0 else below,
            device_id_type=MESH,
        )

    def send_halo(phase, c):
        for side in range(2):
            halo_copy(phase, side, c).start()

    def mean_copy(step, stage, c):
        src, dst, peer = (
            (part.at[step, 2 * c + 1 - core], part_land.at[step, c], twin),
            (pair.at[step, c], pair_land.at[step, c], across),
            (mean.at[step, 2 * c + core], mean.at[step, 2 * c + core], twin),
        )[stage]
        return pltpu.make_async_remote_copy(
            src_ref=src, dst_ref=dst,
            send_sem=mean_send.at[step, stage, c], recv_sem=mean_recv.at[step, stage, c],
            device_id=peer, device_id_type=MESH,
        )

    def start_halo(c, carry):
        send_halo(0, c)
        return carry

    lax.fori_loop(0, CHUNKS, start_halo, 0)

    for load in parcel_loads:
        load.wait()
    parcel_copies = [
        pltpu.make_async_remote_copy(
            src_ref=held.at[f], dst_ref=held.at[f],
            send_sem=parcel_send.at[k, i], recv_sem=parcel_recv.at[k, i],
            device_id=peer, device_id_type=MESH,
        )
        for k, held in enumerate((cells, masses, temps))
        for i, peer in enumerate((twin, across, corner))
    ]
    for copy in parcel_copies:
        copy.start()

    def set_coef(step, sub_step):
        def one(b, carry):
            for p in range(CX):
                for d in range(3):
                    speed = velocity[d, p]
                    drift = (0.5 * noise_gain) * noise[step, sub_step, b, d, p].astype(F32)
                    coef[b, p, 2 * d] = (sub_time * diffusivity) + sub_time * jnp.maximum(speed, 0.0) - drift
                    coef[b, p, 2 * d + 1] = (sub_time * diffusivity) - sub_time * jnp.minimum(speed, 0.0) + drift
            return carry

        lax.fori_loop(0, 2, one, 0)

    loads[0].wait()
    for p in range(CX):
        speeds = jnp.abs(velocity[0, p]) + jnp.abs(velocity[1, p]) + jnp.abs(velocity[2, p])
        coef_mid[p] = (1.0 - 6.0 * sub_time * diffusivity) - sub_time * speeds
    loads[1].wait()
    set_coef(0, 0)
    loads[2].wait()
    loads[3].wait()
    weight[...] = step_time * weight[...]

    def substep(phase, c):
        held, made = ((old, new), (new, old))[phase % 2]

        def one(b, carry):
            for p in range(CX):
                for j in range(2):
                    n = 2 * c + j
                    q = held[b, n, p]
                    lower = held[b, n, p - 1] if p else halo[phase, 0, b, n]
                    upper = held[b, n, p + 1] if p < CX - 1 else halo[phase, 1, b, n]
                    made[b, n, p] = (
                        coef_mid[p] * q
                        + coef[b, p, 0] * lower
                        + coef[b, p, 1] * upper
                        + coef[b, p, 2] * pltpu.roll(q, 1, 0)
                        + coef[b, p, 3] * pltpu.roll(q, NY - 1, 0)
                        + coef[b, p, 4] * pltpu.roll(q, 1, 1)
                        + coef[b, p, 5] * pltpu.roll(q, NZ - 1, 1)
                    )
            return carry

        lax.fori_loop(0, 2, one, 0)

    def evaporate(step):
        stacked = jnp.concatenate(
            [piece for n in range(2) for piece in split3(mean[step, n].reshape(ROWS, NZ))], axis=0
        )
        source[...] = jnp.zeros_like(source)
        per_group = P_DEV // P_BLOCK

        def one(i, carry):
            g = i // per_group
            at = pl.ds(pl.multiple_of(lax.rem(i, per_group) * P_BLOCK, P_BLOCK), P_BLOCK)
            cell = cells[g, :, at]
            in_row = lax.shift_right_logical(cell, 8) == lax.broadcasted_iota(jnp.int32, (ROWS, P_BLOCK), 0)
            in_column = jnp.where(
                (cell & (NZ - 1)) == lax.broadcasted_iota(jnp.int32, (NZ, P_BLOCK), 0), 1.0, 0.0
            ).astype(BF16)
            picked = jnp.dot(stacked, in_column, preferred_element_type=F32)

            def of(n):
                piece = [picked[(3 * n + k) * ROWS:(3 * n + k + 1) * ROWS] for k in range(3)]
                return jnp.sum(jnp.where(in_row, piece[0] + piece[1] + piece[2], 0.0), axis=0, keepdims=True)

            vapor, gas_heat = of(0), of(1)
            mass, temper = masses[g, :, at], temps[g, :, at]
            sat = 0.8 / (1.0 + jnp.exp(-4.0 * (temper - 1.0)))
            drive = jnp.maximum(sat - vapor, 0.0) / (1.0 - sat)
            rate = mass * jnp.log1p(drive)
            heat = rate * (gas_heat - latent_heat)
            masses[g, :, at] = mass - step_time * rate
            temps[g, :, at] = temper + step_time * (gas_heat - temper)
            spread = jnp.concatenate(
                [
                    jnp.where(in_row, piece.astype(F32), 0.0).astype(BF16)
                    for value in (rate, heat)
                    for piece in split3(value)
                ],
                axis=0,
            )
            summed = lax.dot_general(
                spread, in_column, (((1,), (1,)), ((), ())), preferred_element_type=F32
            )
            for n in range(2):
                piece = [summed[(3 * n + k) * ROWS:(3 * n + k + 1) * ROWS] for k in range(3)]
                source[n] += piece[0] + piece[1] + piece[2]
            return carry

        lax.fori_loop(0, GROUPS * per_group, one, 0)

    def sum_parts(step, c):
        def one(p, carry):
            for j in range(2):
                part[step, 2 * c + j, p] = old[0, 2 * c + j, p] + old[1, 2 * c + j, p]
            return carry

        lax.fori_loop(0, CX, one, 0)

    def relax(step, c):
        def one(p, carry):
            for j in range(2):
                for b in range(2):
                    moved = old[b, 2 * c + j, p]
                    old[b, 2 * c + j, p] = moved - weight[p] * (moved - mean[step, 2 * c + j, p])
            return carry

        lax.fori_loop(0, CX, one, 0)

        @pl.when(c == 0)
        def _():
            if step == 0:
                for copy in parcel_copies:
                    copy.wait()
            evaporate(step)
            for j in range(2):
                for p in range(CX):
                    for b in range(2):
                        old[b, j, p] += step_time * source[j, p * NY:(p + 1) * NY]

    def out_copy(c):
        at = pl.ds(2 * c, 2)
        return pltpu.make_async_copy(old.at[:, at], fields_out.at[:, at], out_sem.at[c])

    for step in range(2):
        if step:
            set_coef(step, 0)

        def first(c, carry):
            for side in range(2):
                halo_copy(2 * step, side, c).wait_recv()
                if step:
                    halo_copy(1, side, c).wait_send()
            substep(2 * step, c)
            send_halo(2 * step + 1, c)
            return carry

        lax.fori_loop(0, CHUNKS, first, 0)
        set_coef(step, 1)

        def second(i, carry):
            @pl.when(i < CHUNKS)
            def _():
                c = i
                for side in range(2):
                    halo_copy(2 * step + 1, side, c).wait_recv()
                    if step:
                        halo_copy(2, side, c).wait_send()
                substep(2 * step + 1, c)
                sum_parts(step, c)
                mean_copy(step, 0, c).start()

            @pl.when((i >= 1) & (i < CHUNKS + 1))
            def _():
                c = i - 1
                mean_copy(step, 0, c).wait_recv()
                pair[step, c] = part[step, 2 * c + core] + part_land[step, c]
                mean_copy(step, 1, c).start()

            @pl.when((i >= LAG_TOTAL) & (i < CHUNKS + LAG_TOTAL))
            def _():
                c = i - LAG_TOTAL
                mean_copy(step, 1, c).wait_recv()
                mean[step, 2 * c + core] = 0.125 * (pair[step, c] + pair_land[step, c])
                mean_copy(step, 2, c).start()

            @pl.when(i >= LAG_RELAX)
            def _():
                c = i - LAG_RELAX
                mean_copy(step, 2, c).wait_recv()
                relax(step, c)
                if step == 0:
                    send_halo(2, c)
                else:
                    out_copy(c).start()

            return carry

        lax.fori_loop(0, CHUNKS + LAG_RELAX, second, 0)

    mass_out[...] = masses[f]
    temp_out[...] = temps[f]

    def finish(c, carry):
        for side in range(2):
            halo_copy(0, side, c).wait_send()
            halo_copy(3, side, c).wait_send()
        for step in range(2):
            for stage in range(3):
                mean_copy(step, stage, c).wait_send()
        out_copy(c).wait()
        return carry

    lax.fori_loop(0, CHUNKS, finish, 0)


def on_device(fields, velocity, noise, mixing_rate, parcel_cell, parcel_mass, parcel_temp):
    anywhere = pl.BlockSpec(memory_space=pl.ANY)
    in_vmem = pl.BlockSpec(memory_space=pltpu.VMEM)
    plane = (NY, NZ)
    block = (CX,) + plane
    dma = pltpu.SemaphoreType.DMA
    return pl.pallas_call(
        kernel,
        out_shape=(
            jax.ShapeDtypeStruct(fields.shape, F32),
            jax.ShapeDtypeStruct(parcel_mass.shape, F32),
            jax.ShapeDtypeStruct(parcel_temp.shape, F32),
        ),
        in_specs=[anywhere] * 7,
        out_specs=(anywhere, in_vmem, in_vmem),
        scratch_shapes=[
            pltpu.VMEM((2, S) + block, F32),
            pltpu.VMEM((2, S) + block, F32),
            pltpu.VMEM((4, 2, 2, S) + plane, F32),
            pltpu.VMEM(noise.shape, jnp.int32),
            pltpu.VMEM((3,) + block, F32),
            pltpu.VMEM(block, F32),
            pltpu.VMEM((2, CX, 6) + plane, F32),
            pltpu.VMEM(block, F32),
            pltpu.VMEM((2, S) + block, F32),
            pltpu.VMEM((2, CHUNKS) + block, F32),
            pltpu.VMEM((2, CHUNKS) + block, F32),
            pltpu.VMEM((2, CHUNKS) + block, F32),
            pltpu.VMEM((2, S) + block, F32),
            pltpu.VMEM((2, ROWS, NZ), F32),
            pltpu.VMEM((GROUPS, 1, P_DEV), jnp.int32),
            pltpu.VMEM((GROUPS, 1, P_DEV), F32),
            pltpu.VMEM((GROUPS, 1, P_DEV), F32),
            dma((4,)),
            dma((3,)),
            dma((4, 2, CHUNKS)),
            dma((4, 2, CHUNKS)),
            dma((2, 3, CHUNKS)),
            dma((2, 3, CHUNKS)),
            dma((3, 3)),
            dma((3, 3)),
            dma((CHUNKS,)),
        ],
        compiler_params=pltpu.CompilerParams(
            collective_id=0, has_side_effects=True, vmem_limit_bytes=62 << 20
        ),
    )(fields, velocity, noise, mixing_rate, parcel_cell, parcel_mass, parcel_temp)


def solution(mesh):
    placed = (
        P("field", None, "space", None, None),
        P(None, "space", None, None),
        P(None, None, "field", None, "space", None, None),
        P("space", None, None),
        P("field", "space"),
        P("field", "space"),
        P("field", "space"),
    )
    return jax.shard_map(
        on_device,
        mesh=mesh,
        in_specs=placed,
        out_specs=(P("field", None, "space", None, None), P("field", "space"), P("field", "space")),
        check_vma=False,
    )
```

```python
import jax
import jax.numpy as jnp
from jax import lax
from jax.experimental import pallas as pl
from jax.experimental.pallas import tpu as pltpu
from jax.sharding import PartitionSpec as P

MESH = pl.DeviceIdType.MESH
F32 = jnp.float32
BF16 = jnp.bfloat16

S, CX, NY, NZ = 22, 4, 32, 256
CHUNKS = S // 2
GROUPS, P_DEV = 4, 1024
ROWS = CX * NY
P_BLOCK = 512

sub_time = 0.2
diffusivity = 0.1
noise_gain = 0.2
step_time = 0.4
latent_heat = 0.5

LAG_TOTAL = 3
LAG_RELAX = 4
LAG_PASS = 4


def split3(value):
    top = value.astype(BF16)
    rest = value - top.astype(F32)
    middle = rest.astype(BF16)
    return top, middle, (rest - middle.astype(F32)).astype(BF16)


def kernel(
    fields_in, velocity_in, noise_in, mixing_in, cell_in, mass_in, temp_in,
    old, mass_out, temp_out,
    new, halo, noise, velocity, weight, coef, coef_mid,
    part, part_land, pair, pair_land, mean, source,
    cells, masses, temps,
    load_sem, parcel_load_sem, halo_send, halo_recv, mean_send, mean_recv,
    parcel_send, parcel_recv, relay_send,
):
    f = lax.axis_index("field")
    s = lax.axis_index("space")
    blocks = lax.axis_size("space")
    core = lax.rem(f, 2)
    above = {"space": lax.rem(s + 1, blocks)}
    below = {"space": lax.rem(s + blocks - 1, blocks)}
    twin = {"field": f + 1 - 2 * core}
    across = {"field": lax.rem(f + 2, 4)}
    corner = {"field": 3 - f}

    loads = [
        pltpu.make_async_copy(velocity_in, velocity, load_sem.at[0]),
        pltpu.make_async_copy(noise_in, noise, load_sem.at[1]),
        pltpu.make_async_copy(fields_in, old, load_sem.at[2]),
        pltpu.make_async_copy(mixing_in, weight, load_sem.at[3]),
    ]
    for load in loads:
        load.start()
    parcel_loads = [
        pltpu.make_async_copy(array, held.at[f], parcel_load_sem.at[k])
        for k, (array, held) in enumerate(((cell_in, cells), (mass_in, masses), (temp_in, temps)))
    ]
    for load in parcel_loads:
        load.start()

    base = s - lax.rem(s, 16)
    other = 16 - base
    x = lax.rem(s, 16) // 4
    upward = lax.rem(s, 4) == 3
    downward = lax.rem(s, 4) == 0
    edge = upward | downward
    rank = jnp.where(upward, x, 3 - x)
    is_relay = edge & (rank != 0)
    is_end = edge & (rank == 3)
    relay_side = jnp.where(upward, 0, 1)
    relay_dest = {"space": base + jnp.where(upward, 0, 15)}
    relay_source = {"space": other + jnp.where(upward, 15, 0)}

    barrier = pltpu.get_barrier_semaphore()

    def greet(peer):
        pl.semaphore_signal(barrier, 1, device_id=peer, device_id_type=MESH)

    for peer in (above, below, twin, across, corner):
        greet(peer)

    @pl.when(is_relay)
    def _():
        greet(relay_source)

    @pl.when(is_end)
    def _():
        for column in range(1, 4):
            greet({"space": base + jnp.where(upward, 4 * (3 - column), 4 * column + 3)})

    pl.semaphore_wait(barrier, 5 + jnp.where(is_relay, 1, 0) + jnp.where(is_end, 3, 0))

    def halo_copy(phase, side, c):
        plane = CX - 1 if side == 0 else 0
        held = (fields_in, new, old, new)[phase]
        land, peer = side, (above if side == 0 else below)["space"]
        if phase:
            route = lax.rem(c, 4)
            by_relay = is_end & (upward if side == 0 else downward) & (route != 0)
            land = jnp.where(by_relay, 2, side)
            column = 4 * route + 3 if side == 0 else 4 * (3 - route)
            peer = jnp.where(by_relay, other + column, peer)
        return pltpu.make_async_remote_copy(
            src_ref=held.at[:, pl.ds(2 * c, 2), plane],
            dst_ref=halo.at[phase, land, :, pl.ds(2 * c, 2)],
            send_sem=halo_send.at[phase, side, c],
            recv_sem=halo_recv.at[phase, land, c],
            device_id={"space": peer},
            device_id_type=MESH,
        )

    def halo_arrived(phase, side, c):
        there = halo.at[phase, side, :, pl.ds(2 * c, 2)]
        pltpu.make_async_copy(there, there, halo_recv.at[phase, side, c]).wait()

    def relay_copy(phase, c):
        return pltpu.make_async_remote_copy(
            src_ref=halo.at[phase, 2, :, pl.ds(2 * c, 2)],
            dst_ref=halo.at[phase, relay_side, :, pl.ds(2 * c, 2)],
            send_sem=relay_send.at[phase, c],
            recv_sem=halo_recv.at[phase, relay_side, c],
            device_id=relay_dest,
            device_id_type=MESH,
        )

    def relays(phase, c):
        return is_relay & (lax.rem(c, 4) == rank)

    def pass_on(phase, c):
        @pl.when((c >= 0) & (c < CHUNKS) & relays(phase, c))
        def _():
            halo_arrived(phase, 2, c)
            relay_copy(phase, c).start()

    def send_halo(phase, c):
        for side in range(2):
            halo_copy(phase, side, c).start()

    def mean_copy(step, stage, c):
        src, dst, peer = (
            (part.at[step, 2 * c + 1 - core], part_land.at[step, c], twin),
            (pair.at[step, c], pair_land.at[step, c], across),
            (mean.at[step, 2 * c + core], mean.at[step, 2 * c + core], twin),
        )[stage]
        return pltpu.make_async_remote_copy(
            src_ref=src, dst_ref=dst,
            send_sem=mean_send.at[step, stage, c], recv_sem=mean_recv.at[step, stage, c],
            device_id=peer, device_id_type=MESH,
        )

    def start_halo(c, carry):
        send_halo(0, c)
        return carry

    lax.fori_loop(0, CHUNKS, start_halo, 0)

    for load in parcel_loads:
        load.wait()
    parcel_copies = [
        pltpu.make_async_remote_copy(
            src_ref=held.at[f], dst_ref=held.at[f],
            send_sem=parcel_send.at[k, i], recv_sem=parcel_recv.at[k, i],
            device_id=peer, device_id_type=MESH,
        )
        for k, held in enumerate((cells, masses, temps))
        for i, peer in enumerate((twin, across, corner))
    ]
    for copy in parcel_copies:
        copy.start()

    def set_coef(step, sub_step):
        def one(b, carry):
            for p in range(CX):
                for d in range(3):
                    speed = velocity[d, p]
                    drift = (0.5 * noise_gain) * noise[step, sub_step, b, d, p].astype(F32)
                    coef[b, p, 2 * d] = (sub_time * diffusivity) + sub_time * jnp.maximum(speed, 0.0) - drift
                    coef[b, p, 2 * d + 1] = (sub_time * diffusivity) - sub_time * jnp.minimum(speed, 0.0) + drift
            return carry

        lax.fori_loop(0, 2, one, 0)

    loads[0].wait()
    for p in range(CX):
        speeds = jnp.abs(velocity[0, p]) + jnp.abs(velocity[1, p]) + jnp.abs(velocity[2, p])
        coef_mid[p] = (1.0 - 6.0 * sub_time * diffusivity) - sub_time * speeds
    loads[1].wait()
    set_coef(0, 0)
    loads[2].wait()
    loads[3].wait()
    weight[...] = step_time * weight[...]

    def substep(phase, c):
        held, made = ((old, new), (new, old))[phase % 2]

        def one(b, carry):
            for p in range(CX):
                for j in range(2):
                    n = 2 * c + j
                    q = held[b, n, p]
                    lower = held[b, n, p - 1] if p else halo[phase, 0, b, n]
                    upper = held[b, n, p + 1] if p < CX - 1 else halo[phase, 1, b, n]
                    made[b, n, p] = (
                        coef_mid[p] * q
                        + coef[b, p, 0] * lower
                        + coef[b, p, 1] * upper
                        + coef[b, p, 2] * pltpu.roll(q, 1, 0)
                        + coef[b, p, 3] * pltpu.roll(q, NY - 1, 0)
                        + coef[b, p, 4] * pltpu.roll(q, 1, 1)
                        + coef[b, p, 5] * pltpu.roll(q, NZ - 1, 1)
                    )
            return carry

        lax.fori_loop(0, 2, one, 0)

    def evaporate(step):
        stacked = jnp.concatenate(
            [piece for n in range(2) for piece in split3(mean[step, n].reshape(ROWS, NZ))], axis=0
        )
        source[...] = jnp.zeros_like(source)
        per_group = P_DEV // P_BLOCK

        def one(i, carry):
            g = i // per_group
            at = pl.ds(pl.multiple_of(lax.rem(i, per_group) * P_BLOCK, P_BLOCK), P_BLOCK)
            cell = cells[g, :, at]
            in_row = lax.shift_right_logical(cell, 8) == lax.broadcasted_iota(jnp.int32, (ROWS, P_BLOCK), 0)
            in_column = jnp.where(
                (cell & (NZ - 1)) == lax.broadcasted_iota(jnp.int32, (NZ, P_BLOCK), 0), 1.0, 0.0
            ).astype(BF16)
            picked = jnp.dot(stacked, in_column, preferred_element_type=F32)

            def of(n):
                piece = [picked[(3 * n + k) * ROWS:(3 * n + k + 1) * ROWS] for k in range(3)]
                return jnp.sum(jnp.where(in_row, piece[0] + piece[1] + piece[2], 0.0), axis=0, keepdims=True)

            vapor, gas_heat = of(0), of(1)
            mass, temper = masses[g, :, at], temps[g, :, at]
            sat = 0.8 / (1.0 + jnp.exp(-4.0 * (temper - 1.0)))
            drive = jnp.maximum(sat - vapor, 0.0) / (1.0 - sat)
            rate = mass * jnp.log1p(drive)
            heat = rate * (gas_heat - latent_heat)
            masses[g, :, at] = mass - step_time * rate
            temps[g, :, at] = temper + step_time * (gas_heat - temper)
            spread = jnp.concatenate(
                [
                    jnp.where(in_row, piece.astype(F32), 0.0).astype(BF16)
                    for value in (rate, heat)
                    for piece in split3(value)
                ],
                axis=0,
            )
            summed = lax.dot_general(
                spread, in_column, (((1,), (1,)), ((), ())), preferred_element_type=F32
            )
            for n in range(2):
                piece = [summed[(3 * n + k) * ROWS:(3 * n + k + 1) * ROWS] for k in range(3)]
                source[n] += piece[0] + piece[1] + piece[2]
            return carry

        lax.fori_loop(0, GROUPS * per_group, one, 0)

    def sum_parts(step, c):
        def one(p, carry):
            for j in range(2):
                part[step, 2 * c + j, p] = old[0, 2 * c + j, p] + old[1, 2 * c + j, p]
            return carry

        lax.fori_loop(0, CX, one, 0)

    def relax(step, c):
        def one(p, carry):
            for j in range(2):
                for b in range(2):
                    moved = old[b, 2 * c + j, p]
                    old[b, 2 * c + j, p] = moved - weight[p] * (moved - mean[step, 2 * c + j, p])
            return carry

        lax.fori_loop(0, CX, one, 0)

        @pl.when(c == 0)
        def _():
            if step == 0:
                for copy in parcel_copies:
                    copy.wait()
            evaporate(step)
            for j in range(2):
                for p in range(CX):
                    for b in range(2):
                        old[b, j, p] += step_time * source[j, p * NY:(p + 1) * NY]

    for step in range(2):
        if step:
            set_coef(step, 0)

        def first(c, carry):
            if step:
                pass_on(2, c + CHUNKS - LAG_PASS)
            pass_on(2 * step + 1, c - LAG_PASS)
            for side in range(2):
                halo_arrived(2 * step, side, c)
                if step:
                    halo_copy(1, side, c).wait_send()
            substep(2 * step, c)
            send_halo(2 * step + 1, c)
            return carry

        lax.fori_loop(0, CHUNKS, first, 0)
        set_coef(step, 1)

        def second(i, carry):
            pass_on(2 * step + 1, i + CHUNKS - LAG_PASS)
            if step == 0:
                pass_on(2, i - LAG_RELAX - LAG_PASS)

            @pl.when(i < CHUNKS)
            def _():
                c = i
                for side in range(2):
                    halo_arrived(2 * step + 1, side, c)
                    if step:
                        halo_copy(2, side, c).wait_send()
                substep(2 * step + 1, c)
                sum_parts(step, c)
                mean_copy(step, 0, c).start()

            @pl.when((i >= 1) & (i < CHUNKS + 1))
            def _():
                c = i - 1
                mean_copy(step, 0, c).wait_recv()
                pair[step, c] = part[step, 2 * c + core] + part_land[step, c]
                mean_copy(step, 1, c).start()

            @pl.when((i >= LAG_TOTAL) & (i < CHUNKS + LAG_TOTAL))
            def _():
                c = i - LAG_TOTAL
                mean_copy(step, 1, c).wait_recv()
                mean[step, 2 * c + core] = 0.125 * (pair[step, c] + pair_land[step, c])
                mean_copy(step, 2, c).start()

            @pl.when(i >= LAG_RELAX)
            def _():
                c = i - LAG_RELAX
                mean_copy(step, 2, c).wait_recv()
                relax(step, c)
                if step == 0:
                    send_halo(2, c)

            return carry

        lax.fori_loop(0, CHUNKS + LAG_RELAX, second, 0)

    mass_out[...] = masses[f]
    temp_out[...] = temps[f]

    def finish(c, carry):
        for side in range(2):
            halo_copy(0, side, c).wait_send()
            halo_copy(3, side, c).wait_send()
        for step in range(2):
            for stage in range(3):
                mean_copy(step, stage, c).wait_send()
        for phase in range(1, 4):
            @pl.when(relays(phase, c))
            def _():
                relay_copy(phase, c).wait_send()

        return carry

    lax.fori_loop(0, CHUNKS, finish, 0)


def on_device(fields, velocity, noise, mixing_rate, parcel_cell, parcel_mass, parcel_temp):
    anywhere = pl.BlockSpec(memory_space=pl.ANY)
    in_vmem = pl.BlockSpec(memory_space=pltpu.VMEM)
    plane = (NY, NZ)
    block = (CX,) + plane
    dma = pltpu.SemaphoreType.DMA
    return pl.pallas_call(
        kernel,
        out_shape=(
            pltpu.VMEM(fields.shape, F32),
            pltpu.VMEM(parcel_mass.shape, F32),
            pltpu.VMEM(parcel_temp.shape, F32),
        ),
        in_specs=[anywhere] * 7,
        out_specs=(in_vmem,) * 3,
        scratch_shapes=[
            pltpu.VMEM((2, S) + block, F32),
            pltpu.VMEM((4, 3, 2, S) + plane, F32),
            pltpu.VMEM(noise.shape, jnp.int32),
            pltpu.VMEM((3,) + block, F32),
            pltpu.VMEM(block, F32),
            pltpu.VMEM((2, CX, 6) + plane, F32),
            pltpu.VMEM(block, F32),
            pltpu.VMEM((2, S) + block, F32),
            pltpu.VMEM((2, CHUNKS) + block, F32),
            pltpu.VMEM((2, CHUNKS) + block, F32),
            pltpu.VMEM((2, CHUNKS) + block, F32),
            pltpu.VMEM((2, S) + block, F32),
            pltpu.VMEM((2, ROWS, NZ), F32),
            pltpu.VMEM((GROUPS, 1, P_DEV), jnp.int32),
            pltpu.VMEM((GROUPS, 1, P_DEV), F32),
            pltpu.VMEM((GROUPS, 1, P_DEV), F32),
            dma((4,)),
            dma((3,)),
            dma((4, 2, CHUNKS)),
            dma((4, 3, CHUNKS)),
            dma((2, 3, CHUNKS)),
            dma((2, 3, CHUNKS)),
            dma((3, 3)),
            dma((3, 3)),
            dma((4, CHUNKS)),
        ],
        compiler_params=pltpu.CompilerParams(
            collective_id=0, has_side_effects=True, vmem_limit_bytes=57 << 20
        ),
    )(fields, velocity, noise, mixing_rate, parcel_cell, parcel_mass, parcel_temp)


def solution(mesh):
    placed = (
        P("field", None, "space", None, None),
        P(None, "space", None, None),
        P(None, None, "field", None, "space", None, None),
        P("space", None, None),
        P("field", "space"),
        P("field", "space"),
        P("field", "space"),
    )
    return jax.shard_map(
        on_device,
        mesh=mesh,
        in_specs=placed,
        out_specs=(P("field", None, "space", None, None), P("field", "space"), P("field", "space")),
        check_vma=False,
    )
```

```python
import jax
import jax.numpy as jnp
from jax import lax
from jax.experimental import pallas as pl
from jax.experimental.pallas import tpu as pltpu
from jax.sharding import PartitionSpec as P

MESH = pl.DeviceIdType.MESH
F32 = jnp.float32
BF16 = jnp.bfloat16

S, CX, NY, NZ = 22, 4, 32, 256
CHUNKS = S // 2
GROUPS, P_DEV = 4, 1024
ROWS = CX * NY
P_BLOCK = 512

sub_time = 0.2
diffusivity = 0.1
noise_gain = 0.2
step_time = 0.4
latent_heat = 0.5

FIRST_GROUP = 5
LAG_PAIR = 1
LAG_TOTAL = 2
LAG_RELAX = 3
LAG_PASS = 2
WINDOW = 3


def split3(value):
    top = value.astype(BF16)
    rest = value - top.astype(F32)
    middle = rest.astype(BF16)
    return top, middle, (rest - middle.astype(F32)).astype(BF16)


def kernel(
    fields_in, velocity_in, noise_in, mixing_in, cell_in, mass_in, temp_in,
    old, mass_out, temp_out,
    new, halo, noise, velocity, weight, coef, coef_mid,
    part, part_land, pair, pair_land, mean, source,
    cells, masses, temps,
    load_sem, parcel_load_sem, halo_send, halo_recv, mean_send, mean_recv,
    parcel_send, parcel_recv, relay_send,
):
    f = lax.axis_index("field")
    s = lax.axis_index("space")
    blocks = lax.axis_size("space")
    core = lax.rem(f, 2)
    above = {"space": lax.rem(s + 1, blocks)}
    below = {"space": lax.rem(s + blocks - 1, blocks)}
    twin = {"field": f + 1 - 2 * core}
    across = {"field": lax.rem(f + 2, 4)}
    corner = {"field": 3 - f}

    loads = [
        pltpu.make_async_copy(velocity_in, velocity, load_sem.at[0]),
        pltpu.make_async_copy(noise_in, noise, load_sem.at[1]),
        pltpu.make_async_copy(fields_in, old, load_sem.at[2]),
        pltpu.make_async_copy(mixing_in, weight, load_sem.at[3]),
    ]
    for load in loads:
        load.start()
    parcel_loads = [
        pltpu.make_async_copy(array, held.at[f], parcel_load_sem.at[k])
        for k, (array, held) in enumerate(((cell_in, cells), (mass_in, masses), (temp_in, temps)))
    ]
    for load in parcel_loads:
        load.start()

    base = s - lax.rem(s, 16)
    other = 16 - base
    place = lax.rem(s, 16)
    upward = place == 15
    downward = place == 0
    is_end = upward | downward
    relay_side = jnp.where(upward, 0, 1)
    relay_dest = {"space": base + jnp.where(upward, 0, 15)}
    relay_peer = {"space": other + place}

    barrier = pltpu.get_barrier_semaphore()

    def greet(peer):
        pl.semaphore_signal(barrier, 1, device_id=peer, device_id_type=MESH)

    for peer in (above, below, twin, across, corner):
        greet(peer)

    @pl.when(is_end)
    def _():
        greet(relay_peer)
        greet(relay_dest)

    pl.semaphore_wait(barrier, 5 + jnp.where(is_end, 2, 0))

    def goes_round(phase, c):
        if phase == 1:
            return c >= 0
        if phase == 3:
            return c >= 0
        return c < 0

    def halo_copy(phase, side, c):
        plane = CX - 1 if side == 0 else 0
        held = (fields_in, new, old, new)[phase]
        land, peer = side, (above if side == 0 else below)["space"]
        relayed = by_relay(phase, side, c)
        land = jnp.where(relayed, 2, side)
        peer = jnp.where(relayed, other + (15 if side == 0 else 0), peer)
        return pltpu.make_async_remote_copy(
            src_ref=held.at[:, pl.ds(2 * c, 2), plane],
            dst_ref=halo.at[phase, land, :, pl.ds(2 * c, 2)],
            send_sem=halo_send.at[phase, side, c],
            recv_sem=halo_recv.at[phase, land, c],
            device_id={"space": peer},
            device_id_type=MESH,
        )

    def halo_arrived(phase, side, c):
        there = halo.at[phase, side, :, pl.ds(2 * c, 2)]
        pltpu.make_async_copy(there, there, halo_recv.at[phase, side, c]).wait()

    def relay_copy(phase, c):
        return pltpu.make_async_remote_copy(
            src_ref=halo.at[phase, 2, :, pl.ds(2 * c, 2)],
            dst_ref=halo.at[phase, relay_side, :, pl.ds(2 * c, 2)],
            send_sem=relay_send.at[phase, c],
            recv_sem=halo_recv.at[phase, relay_side, c],
            device_id=relay_dest,
            device_id_type=MESH,
        )

    def relays(phase, c):
        return is_end & goes_round(phase, c)

    def pass_on(phase, c):
        @pl.when(relays(phase, c))
        def _():
            halo_arrived(phase, 2, c)
            relay_copy(phase, c).start()

    def by_relay(phase, side, c):
        return is_end & (upward if side == 0 else downward) & goes_round(phase, c)

    def send_early(phase, c):
        for side in range(2):
            @pl.when(by_relay(phase, side, c))
            def _():
                halo_copy(phase, side, c).start()

    def send_in_turn(phase, c):
        for side in range(2):
            @pl.when(jnp.logical_not(by_relay(phase, side, c)))
            def _():
                halo_copy(phase, side, c).start()

    def mean_copy(step, stage, c):
        src, dst, peer = (
            (part.at[step, 2 * c + 1 - core], part_land.at[step, c], twin),
            (pair.at[step, c], pair_land.at[step, c], across),
            (mean.at[step, 2 * c + core], mean.at[step, 2 * c + core], twin),
        )[stage]
        return pltpu.make_async_remote_copy(
            src_ref=src, dst_ref=dst,
            send_sem=mean_send.at[step, stage, c], recv_sem=mean_recv.at[step, stage, c],
            device_id=peer, device_id_type=MESH,
        )

    def start_halo(c, carry):
        send_in_turn(0, c)
        return carry

    lax.fori_loop(0, FIRST_GROUP, start_halo, 0)

    for load in parcel_loads:
        load.wait()
    parcel_copies = [
        pltpu.make_async_remote_copy(
            src_ref=held.at[f], dst_ref=held.at[f],
            send_sem=parcel_send.at[k, i], recv_sem=parcel_recv.at[k, i],
            device_id=peer, device_id_type=MESH,
        )
        for k, held in enumerate((cells, masses, temps))
        for i, peer in enumerate((twin, across, corner))
    ]
    for copy in parcel_copies:
        copy.start()

    def set_coef(phase):
        step, sub_step = phase // 2, phase % 2

        def one(b, carry):
            for p in range(CX):
                for d in range(3):
                    speed = velocity[d, p]
                    drift = (0.5 * noise_gain) * noise[step, sub_step, b, d, p].astype(F32)
                    coef[sub_step, b, p, 2 * d] = (sub_time * diffusivity) + sub_time * jnp.maximum(speed, 0.0) - drift
                    coef[sub_step, b, p, 2 * d + 1] = (sub_time * diffusivity) - sub_time * jnp.minimum(speed, 0.0) + drift
            return carry

        lax.fori_loop(0, 2, one, 0)

    loads[0].wait()
    for p in range(CX):
        speeds = jnp.abs(velocity[0, p]) + jnp.abs(velocity[1, p]) + jnp.abs(velocity[2, p])
        coef_mid[p] = (1.0 - 6.0 * sub_time * diffusivity) - sub_time * speeds
    loads[1].wait()
    set_coef(0)
    loads[2].wait()
    loads[3].wait()
    weight[...] = step_time * weight[...]

    def substep(phase, c):
        held, made = ((old, new), (new, old))[phase % 2]

        def one(b, carry):
            for p in range(CX):
                for j in range(2):
                    n = 2 * c + j
                    q = held[b, n, p]
                    lower = held[b, n, p - 1] if p else halo[phase, 0, b, n]
                    upper = held[b, n, p + 1] if p < CX - 1 else halo[phase, 1, b, n]
                    made[b, n, p] = (
                        coef_mid[p] * q
                        + coef[phase % 2, b, p, 0] * lower
                        + coef[phase % 2, b, p, 1] * upper
                        + coef[phase % 2, b, p, 2] * pltpu.roll(q, 1, 0)
                        + coef[phase % 2, b, p, 3] * pltpu.roll(q, NY - 1, 0)
                        + coef[phase % 2, b, p, 4] * pltpu.roll(q, 1, 1)
                        + coef[phase % 2, b, p, 5] * pltpu.roll(q, NZ - 1, 1)
                    )
            return carry

        lax.fori_loop(0, 2, one, 0)

    def evaporate(step):
        stacked = jnp.concatenate(
            [piece for n in range(2) for piece in split3(mean[step, n].reshape(ROWS, NZ))], axis=0
        )
        source[...] = jnp.zeros_like(source)
        per_group = P_DEV // P_BLOCK

        def one(i, carry):
            g = i // per_group
            at = pl.ds(pl.multiple_of(lax.rem(i, per_group) * P_BLOCK, P_BLOCK), P_BLOCK)
            cell = cells[g, :, at]
            in_row = lax.shift_right_logical(cell, 8) == lax.broadcasted_iota(jnp.int32, (ROWS, P_BLOCK), 0)
            in_column = jnp.where(
                (cell & (NZ - 1)) == lax.broadcasted_iota(jnp.int32, (NZ, P_BLOCK), 0), 1.0, 0.0
            ).astype(BF16)
            picked = jnp.dot(stacked, in_column, preferred_element_type=F32)

            def of(n):
                piece = [picked[(3 * n + k) * ROWS:(3 * n + k + 1) * ROWS] for k in range(3)]
                return jnp.sum(jnp.where(in_row, piece[0] + piece[1] + piece[2], 0.0), axis=0, keepdims=True)

            vapor, gas_heat = of(0), of(1)
            mass, temper = masses[g, :, at], temps[g, :, at]
            sat = 0.8 / (1.0 + jnp.exp(-4.0 * (temper - 1.0)))
            drive = jnp.maximum(sat - vapor, 0.0) / (1.0 - sat)
            rate = mass * jnp.log1p(drive)
            heat = rate * (gas_heat - latent_heat)
            masses[g, :, at] = mass - step_time * rate
            temps[g, :, at] = temper + step_time * (gas_heat - temper)
            spread = jnp.concatenate(
                [
                    jnp.where(in_row, piece.astype(F32), 0.0).astype(BF16)
                    for value in (rate, heat)
                    for piece in split3(value)
                ],
                axis=0,
            )
            summed = lax.dot_general(
                spread, in_column, (((1,), (1,)), ((), ())), preferred_element_type=F32
            )
            for n in range(2):
                piece = [summed[(3 * n + k) * ROWS:(3 * n + k + 1) * ROWS] for k in range(3)]
                source[n] += piece[0] + piece[1] + piece[2]
            return carry

        lax.fori_loop(0, GROUPS * per_group, one, 0)

    def sum_parts(step, c):
        def one(p, carry):
            for j in range(2):
                part[step, 2 * c + j, p] = old[0, 2 * c + j, p] + old[1, 2 * c + j, p]
            return carry

        lax.fori_loop(0, CX, one, 0)

    def relax(step, c):
        def one(p, carry):
            for j in range(2):
                for b in range(2):
                    moved = old[b, 2 * c + j, p]
                    old[b, 2 * c + j, p] = moved - weight[p] * (moved - mean[step, 2 * c + j, p])
            return carry

        lax.fori_loop(0, CX, one, 0)

        @pl.when(c == 0)
        def _():
            if step == 0:
                for copy in parcel_copies:
                    copy.wait()
            evaporate(step)
            for j in range(2):
                for p in range(CX):
                    for b in range(2):
                        old[b, j, p] += step_time * source[j, p * NY:(p + 1) * NY]

    def mean_stages(step, group, at):
        start, count = group

        @pl.when((at >= LAG_PAIR) & (at < count + LAG_PAIR))
        def _():
            c = start + at - LAG_PAIR
            mean_copy(step, 0, c).wait_recv()
            pair[step, c] = part[step, 2 * c + core] + part_land[step, c]
            mean_copy(step, 1, c).start()

        @pl.when((at >= LAG_TOTAL) & (at < count + LAG_TOTAL))
        def _():
            c = start + at - LAG_TOTAL
            mean_copy(step, 1, c).wait_recv()
            mean[step, 2 * c + core] = 0.125 * (pair[step, c] + pair_land[step, c])
            mean_copy(step, 2, c).start()

        @pl.when((at >= LAG_RELAX) & (at < count + LAG_RELAX))
        def _():
            c = start + at - LAG_RELAX
            mean_copy(step, 2, c).wait_recv()
            relax(step, c)

    def guarded(group, j, act, *phase):
        start, count = group

        @pl.when((j >= 0) & (j < count))
        def _():
            act(*phase, start + j)

    def consume(phase, c):
        for side in range(2):
            halo_arrived(phase, side, c)
            if phase >= 2:
                halo_copy(phase - 1, side, c).wait_send()
        substep(phase, c)
        if phase % 2:
            sum_parts(phase // 2, c)
            mean_copy(phase // 2, 0, c).start()
        else:
            send_early(phase + 1, c)

    low, high = (0, FIRST_GROUP), (FIRST_GROUP, CHUNKS - FIRST_GROUP)
    plan = (((0, low),), ((1, low), (0, high)), ((1, high), (2, low)), ((3, low), (2, high)), ((3, high),))
    length = [max(group[1] for _, group in stage) for stage in plan]

    for k, stage in enumerate(plan):
        before = plan[k - 1] if k else ()
        after = plan[k + 1] if k + 1 < len(plan) else ()
        if 1 <= k <= 3:
            set_coef(k)
        if not after:
            for c in range(high[0] + WINDOW, CHUNKS):
                send_in_turn(3, c)

        def body(i, carry):
            for phase, group in before:
                if phase % 2 == 0:
                    guarded(group, i + length[k - 1] - LAG_PASS, pass_on, phase + 1)
            for phase, group in stage:
                if phase % 2 == 0:
                    guarded(group, i - LAG_PASS, pass_on, phase + 1)
            for phase, group in before:
                if phase % 2:
                    mean_stages(phase // 2, group, i + length[k - 1])
            for phase, group in stage:
                guarded(group, i, consume, phase)
                if phase % 2:
                    mean_stages(phase // 2, group, i)
            if 0 < k < len(plan) - 1:
                @pl.when(i < length[k] - WINDOW)
                def _():
                    for phase, group in stage:
                        guarded(group, i + WINDOW, send_in_turn, phase)
            if after:
                @pl.when(i >= length[k] - WINDOW)
                def _():
                    for phase, group in after:
                        guarded(group, i + WINDOW - length[k], send_in_turn, phase)
            return carry

        lax.fori_loop(0, length[k], body, 0)

    def drain(i, carry):
        mean_stages(1, high, i + length[-1])
        return carry

    lax.fori_loop(0, LAG_RELAX, drain, 0)

    mass_out[...] = masses[f]
    temp_out[...] = temps[f]

    def finish(c, carry):
        for side in range(2):
            halo_copy(0, side, c).wait_send()
            halo_copy(3, side, c).wait_send()
        for step in range(2):
            for stage in range(3):
                mean_copy(step, stage, c).wait_send()
        for phase in (1, 3):
            @pl.when(relays(phase, c))
            def _():
                relay_copy(phase, c).wait_send()

        return carry

    lax.fori_loop(0, CHUNKS, finish, 0)


def on_device(fields, velocity, noise, mixing_rate, parcel_cell, parcel_mass, parcel_temp):
    anywhere = pl.BlockSpec(memory_space=pl.ANY)
    in_vmem = pl.BlockSpec(memory_space=pltpu.VMEM)
    plane = (NY, NZ)
    block = (CX,) + plane
    dma = pltpu.SemaphoreType.DMA
    return pl.pallas_call(
        kernel,
        out_shape=(
            pltpu.VMEM(fields.shape, F32),
            pltpu.VMEM(parcel_mass.shape, F32),
            pltpu.VMEM(parcel_temp.shape, F32),
        ),
        in_specs=[anywhere] * 7,
        out_specs=(in_vmem,) * 3,
        scratch_shapes=[
            pltpu.VMEM((2, S) + block, F32),
            pltpu.VMEM((4, 3, 2, S) + plane, F32),
            pltpu.VMEM(noise.shape, jnp.int32),
            pltpu.VMEM((3,) + block, F32),
            pltpu.VMEM(block, F32),
            pltpu.VMEM((2, 2, CX, 6) + plane, F32),
            pltpu.VMEM(block, F32),
            pltpu.VMEM((2, S) + block, F32),
            pltpu.VMEM((2, CHUNKS) + block, F32),
            pltpu.VMEM((2, CHUNKS) + block, F32),
            pltpu.VMEM((2, CHUNKS) + block, F32),
            pltpu.VMEM((2, S) + block, F32),
            pltpu.VMEM((2, ROWS, NZ), F32),
            pltpu.VMEM((GROUPS, 1, P_DEV), jnp.int32),
            pltpu.VMEM((GROUPS, 1, P_DEV), F32),
            pltpu.VMEM((GROUPS, 1, P_DEV), F32),
            dma((4,)),
            dma((3,)),
            dma((4, 2, CHUNKS)),
            dma((4, 3, CHUNKS)),
            dma((2, 3, CHUNKS)),
            dma((2, 3, CHUNKS)),
            dma((3, 3)),
            dma((3, 3)),
            dma((4, CHUNKS)),
        ],
        compiler_params=pltpu.CompilerParams(
            collective_id=0, has_side_effects=True, vmem_limit_bytes=57 << 20
        ),
    )(fields, velocity, noise, mixing_rate, parcel_cell, parcel_mass, parcel_temp)


def solution(mesh):
    placed = (
        P("field", None, "space", None, None),
        P(None, "space", None, None),
        P(None, None, "field", None, "space", None, None),
        P("space", None, None),
        P("field", "space"),
        P("field", "space"),
        P("field", "space"),
    )
    return jax.shard_map(
        on_device,
        mesh=mesh,
        in_specs=placed,
        out_specs=(P("field", None, "space", None, None), P("field", "space"), P("field", "space")),
        check_vma=False,
    )
```

```python
import jax
import jax.numpy as jnp
from jax import lax
from jax.experimental import pallas as pl
from jax.experimental.pallas import tpu as pltpu
from jax.sharding import PartitionSpec as P

MESH = pl.DeviceIdType.MESH
F32 = jnp.float32
BF16 = jnp.bfloat16

S, CX, NY, NZ = 22, 4, 32, 256
CHUNKS = S // 2
GROUPS, P_DEV = 4, 1024
ROWS = CX * NY
P_BLOCK = 512

sub_time = 0.2
diffusivity = 0.1
noise_gain = 0.2
step_time = 0.4
latent_heat = 0.5

FIRST_GROUP = 5
LAG_PAIR = 1
LAG_TOTAL = 2
LAG_RELAX = 3
LAG_PASS = 2
WINDOW = 3


def split3(value):
    top = value.astype(BF16)
    rest = value - top.astype(F32)
    middle = rest.astype(BF16)
    return top, middle, (rest - middle.astype(F32)).astype(BF16)


def kernel(
    fields_in, velocity_in, noise_in, mixing_in, cell_in, mass_in, temp_in,
    old, mass_out, temp_out,
    new, halo, noise, velocity, weight, coef, coef_mid,
    part, part_land, pair, pair_land, mean, source,
    cells, masses, temps,
    load_sem, parcel_load_sem, halo_send, halo_recv, mean_send, mean_recv,
    parcel_send, parcel_recv, relay_send,
):
    f = lax.axis_index("field")
    s = lax.axis_index("space")
    blocks = lax.axis_size("space")
    core = lax.rem(f, 2)
    above = {"space": lax.rem(s + 1, blocks)}
    below = {"space": lax.rem(s + blocks - 1, blocks)}
    twin = {"field": f + 1 - 2 * core}
    across = {"field": lax.rem(f + 2, 4)}
    corner = {"field": 3 - f}

    loads = [
        pltpu.make_async_copy(velocity_in, velocity, load_sem.at[0]),
        pltpu.make_async_copy(noise_in, noise, load_sem.at[1]),
        pltpu.make_async_copy(fields_in, old, load_sem.at[2]),
        pltpu.make_async_copy(mixing_in, weight, load_sem.at[3]),
    ]
    for load in loads:
        load.start()
    parcel_loads = [
        pltpu.make_async_copy(array, held.at[f], parcel_load_sem.at[k])
        for k, (array, held) in enumerate(((cell_in, cells), (mass_in, masses), (temp_in, temps)))
    ]
    for load in parcel_loads:
        load.start()

    base = s - lax.rem(s, 16)
    other = 16 - base
    place = lax.rem(s, 16)
    upward = place == 15
    downward = place == 0
    is_end = upward | downward
    relay_side = jnp.where(upward, 0, 1)
    relay_dest = {"space": base + jnp.where(upward, 0, 15)}
    relay_peer = {"space": other + place}

    barrier = pltpu.get_barrier_semaphore()

    def greet(peer):
        pl.semaphore_signal(barrier, 1, device_id=peer, device_id_type=MESH)

    for peer in (above, below, twin, across, corner):
        greet(peer)

    @pl.when(is_end)
    def _():
        greet(relay_peer)
        greet(relay_dest)

    pl.semaphore_wait(barrier, 5 + jnp.where(is_end, 2, 0))

    def goes_round(phase, c):
        if phase == 1:
            return c >= 0
        if phase == 3:
            return c >= 0
        return c < 0

    def halo_copy(phase, side, c):
        plane = CX - 1 if side == 0 else 0
        held = (fields_in, new, old, new)[phase]
        land, peer = side, (above if side == 0 else below)["space"]
        relayed = by_relay(phase, side, c)
        land = jnp.where(relayed, 2, side)
        peer = jnp.where(relayed, other + (15 if side == 0 else 0), peer)
        return pltpu.make_async_remote_copy(
            src_ref=held.at[:, pl.ds(2 * c, 2), plane],
            dst_ref=halo.at[phase, land, :, pl.ds(2 * c, 2)],
            send_sem=halo_send.at[phase, side, c],
            recv_sem=halo_recv.at[phase, land, c],
            device_id={"space": peer},
            device_id_type=MESH,
        )

    def halo_arrived(phase, side, c):
        there = halo.at[phase, side, :, pl.ds(2 * c, 2)]
        pltpu.make_async_copy(there, there, halo_recv.at[phase, side, c]).wait()

    def relay_copy(phase, c):
        return pltpu.make_async_remote_copy(
            src_ref=halo.at[phase, 2, :, pl.ds(2 * c, 2)],
            dst_ref=halo.at[phase, relay_side, :, pl.ds(2 * c, 2)],
            send_sem=relay_send.at[phase, c],
            recv_sem=halo_recv.at[phase, relay_side, c],
            device_id=relay_dest,
            device_id_type=MESH,
        )

    def relays(phase, c):
        return is_end & goes_round(phase, c)

    def pass_on(phase, c):
        @pl.when(relays(phase, c))
        def _():
            halo_arrived(phase, 2, c)
            relay_copy(phase, c).start()

    def by_relay(phase, side, c):
        return is_end & (upward if side == 0 else downward) & goes_round(phase, c)

    def send_early(phase, c):
        for side in range(2):
            @pl.when(by_relay(phase, side, c))
            def _():
                halo_copy(phase, side, c).start()

    def send_in_turn(phase, c):
        for side in range(2):
            @pl.when(jnp.logical_not(by_relay(phase, side, c)))
            def _():
                halo_copy(phase, side, c).start()

    def mean_copy(step, stage, c):
        src, dst, peer = (
            (part.at[step, 2 * c + 1 - core], part_land.at[step, c], twin),
            (pair.at[step, c], pair_land.at[step, c], across),
            (mean.at[step, 2 * c + core], mean.at[step, 2 * c + core], twin),
        )[stage]
        return pltpu.make_async_remote_copy(
            src_ref=src, dst_ref=dst,
            send_sem=mean_send.at[step, stage, c], recv_sem=mean_recv.at[step, stage, c],
            device_id=peer, device_id_type=MESH,
        )

    def start_halo(c, carry):
        send_in_turn(0, c)
        return carry

    lax.fori_loop(0, FIRST_GROUP, start_halo, 0)

    for load in parcel_loads:
        load.wait()
    parcel_copies = [
        pltpu.make_async_remote_copy(
            src_ref=held.at[f], dst_ref=held.at[f],
            send_sem=parcel_send.at[k, i], recv_sem=parcel_recv.at[k, i],
            device_id=peer, device_id_type=MESH,
        )
        for k, held in enumerate((cells, masses, temps))
        for i, peer in enumerate((twin, across, corner))
    ]
    for copy in parcel_copies:
        copy.start()

    def set_coef(phase):
        step, sub_step = phase // 2, phase % 2

        def one(b, carry):
            for p in range(CX):
                for d in range(3):
                    speed = velocity[d, p]
                    drift = (0.5 * noise_gain) * noise[step, sub_step, b, d, p].astype(F32)
                    coef[sub_step, b, p, 2 * d] = (sub_time * diffusivity) + sub_time * jnp.maximum(speed, 0.0) - drift
                    coef[sub_step, b, p, 2 * d + 1] = (sub_time * diffusivity) - sub_time * jnp.minimum(speed, 0.0) + drift
            return carry

        lax.fori_loop(0, 2, one, 0)

    loads[0].wait()
    for p in range(CX):
        speeds = jnp.abs(velocity[0, p]) + jnp.abs(velocity[1, p]) + jnp.abs(velocity[2, p])
        coef_mid[p] = (1.0 - 6.0 * sub_time * diffusivity) - sub_time * speeds
    loads[1].wait()
    set_coef(0)
    loads[2].wait()
    loads[3].wait()
    weight[...] = step_time * weight[...]

    def substep(phase, c):
        held, made = ((old, new), (new, old))[phase % 2]

        def one(b, carry):
            for p in range(CX):
                for j in range(2):
                    n = 2 * c + j
                    q = held[b, n, p]
                    lower = held[b, n, p - 1] if p else halo[phase, 0, b, n]
                    upper = held[b, n, p + 1] if p < CX - 1 else halo[phase, 1, b, n]
                    made[b, n, p] = (
                        coef_mid[p] * q
                        + coef[phase % 2, b, p, 0] * lower
                        + coef[phase % 2, b, p, 1] * upper
                        + coef[phase % 2, b, p, 2] * pltpu.roll(q, 1, 0)
                        + coef[phase % 2, b, p, 3] * pltpu.roll(q, NY - 1, 0)
                        + coef[phase % 2, b, p, 4] * pltpu.roll(q, 1, 1)
                        + coef[phase % 2, b, p, 5] * pltpu.roll(q, NZ - 1, 1)
                    )
            return carry

        lax.fori_loop(0, 2, one, 0)

    def evaporate(step):
        stacked = jnp.concatenate(
            [piece for n in range(2) for piece in split3(mean[step, n].reshape(ROWS, NZ))], axis=0
        )
        source[...] = jnp.zeros_like(source)
        per_group = P_DEV // P_BLOCK

        def one(i, carry):
            g = i // per_group
            at = pl.ds(pl.multiple_of(lax.rem(i, per_group) * P_BLOCK, P_BLOCK), P_BLOCK)
            cell = cells[g, :, at]
            in_row = lax.shift_right_logical(cell, 8) == lax.broadcasted_iota(jnp.int32, (ROWS, P_BLOCK), 0)
            in_column = jnp.where(
                (cell & (NZ - 1)) == lax.broadcasted_iota(jnp.int32, (NZ, P_BLOCK), 0), 1.0, 0.0
            ).astype(BF16)
            picked = jnp.dot(stacked, in_column, preferred_element_type=F32)

            def of(n):
                piece = [picked[(3 * n + k) * ROWS:(3 * n + k + 1) * ROWS] for k in range(3)]
                return jnp.sum(jnp.where(in_row, piece[0] + piece[1] + piece[2], 0.0), axis=0, keepdims=True)

            vapor, gas_heat = of(0), of(1)
            mass, temper = masses[g, :, at], temps[g, :, at]
            sat = 0.8 / (1.0 + jnp.exp(-4.0 * (temper - 1.0)))
            drive = jnp.maximum(sat - vapor, 0.0) / (1.0 - sat)
            rate = mass * jnp.log1p(drive)
            heat = rate * (gas_heat - latent_heat)
            masses[g, :, at] = mass - step_time * rate
            temps[g, :, at] = temper + step_time * (gas_heat - temper)
            spread = jnp.concatenate(
                [
                    jnp.where(in_row, piece.astype(F32), 0.0).astype(BF16)
                    for value in (rate, heat)
                    for piece in split3(value)
                ],
                axis=0,
            )
            summed = lax.dot_general(
                spread, in_column, (((1,), (1,)), ((), ())), preferred_element_type=F32
            )
            for n in range(2):
                piece = [summed[(3 * n + k) * ROWS:(3 * n + k + 1) * ROWS] for k in range(3)]
                source[n] += piece[0] + piece[1] + piece[2]
            return carry

        lax.fori_loop(0, GROUPS * per_group, one, 0)

    def sum_parts(step, c):
        def one(p, carry):
            for j in range(2):
                part[step, 2 * c + j, p] = old[0, 2 * c + j, p] + old[1, 2 * c + j, p]
            return carry

        lax.fori_loop(0, CX, one, 0)

    def relax(step, c):
        def one(p, carry):
            for j in range(2):
                for b in range(2):
                    moved = old[b, 2 * c + j, p]
                    old[b, 2 * c + j, p] = moved - weight[p] * (moved - mean[step, 2 * c + j, p])
            return carry

        lax.fori_loop(0, CX, one, 0)

        @pl.when(c == 0)
        def _():
            if step == 0:
                for copy in parcel_copies:
                    copy.wait()
            evaporate(step)
            for j in range(2):
                for p in range(CX):
                    for b in range(2):
                        old[b, j, p] += step_time * source[j, p * NY:(p + 1) * NY]

    def mean_stages(step, group, at):
        start, count = group

        @pl.when((at >= LAG_PAIR) & (at < count + LAG_PAIR))
        def _():
            c = start + at - LAG_PAIR
            mean_copy(step, 0, c).wait_recv()
            pair[step, c] = part[step, 2 * c + core] + part_land[step, c]
            mean_copy(step, 1, c).start()

        @pl.when((at >= LAG_TOTAL) & (at < count + LAG_TOTAL))
        def _():
            c = start + at - LAG_TOTAL
            mean_copy(step, 1, c).wait_recv()
            mean[step, 2 * c + core] = 0.125 * (pair[step, c] + pair_land[step, c])
            mean_copy(step, 2, c).start()

        @pl.when((at >= LAG_RELAX) & (at < count + LAG_RELAX))
        def _():
            c = start + at - LAG_RELAX
            mean_copy(step, 2, c).wait_recv()
            relax(step, c)

    def guarded(group, j, act, *phase):
        start, count = group

        @pl.when((j >= 0) & (j < count))
        def _():
            act(*phase, start + j)

    def consume(phase, c):
        for side in range(2):
            halo_arrived(phase, side, c)
            if phase >= 2:
                halo_copy(phase - 1, side, c).wait_send()
        substep(phase, c)
        if phase % 2:
            sum_parts(phase // 2, c)
            mean_copy(phase // 2, 0, c).start()
        else:
            send_early(phase + 1, c)

    low, high = (0, FIRST_GROUP), (FIRST_GROUP, CHUNKS - FIRST_GROUP)
    plan = (((0, low),), ((1, low), (0, high)), ((1, high), (2, low)), ((3, low), (2, high)), ((3, high),))
    length = [max(group[1] for _, group in stage) for stage in plan]

    for k, stage in enumerate(plan):
        before = plan[k - 1] if k else ()
        after = plan[k + 1] if k + 1 < len(plan) else ()
        if 1 <= k <= 3:
            set_coef(k)
        if not after:
            for c in range(high[0] + WINDOW, CHUNKS):
                send_in_turn(3, c)

        def body(i, carry):
            for phase, group in before:
                if phase % 2 == 0:
                    guarded(group, i + length[k - 1] - LAG_PASS, pass_on, phase + 1)
            for phase, group in stage:
                if phase % 2 == 0:
                    guarded(group, i - LAG_PASS, pass_on, phase + 1)
            for phase, group in before:
                if phase % 2:
                    mean_stages(phase // 2, group, i + length[k - 1])
            for phase, group in stage:
                guarded(group, i, consume, phase)
                if phase % 2:
                    mean_stages(phase // 2, group, i)
            if 0 < k < len(plan) - 1:
                @pl.when(i < length[k] - WINDOW)
                def _():
                    for phase, group in stage:
                        guarded(group, i + WINDOW, send_in_turn, phase)
            if after:
                @pl.when(i >= length[k] - WINDOW)
                def _():
                    for phase, group in after:
                        guarded(group, i + WINDOW - length[k], send_in_turn, phase)
            return carry

        lax.fori_loop(0, length[k], body, 0)

    def drain(i, carry):
        mean_stages(1, high, i + length[-1])
        return carry

    lax.fori_loop(0, LAG_RELAX, drain, 0)

    mass_out[...] = masses[f]
    temp_out[...] = temps[f]

    def finish(c, carry):
        for side in range(2):
            halo_copy(0, side, c).wait_send()
            halo_copy(3, side, c).wait_send()
        for step in range(2):
            for stage in range(3):
                mean_copy(step, stage, c).wait_send()
        for phase in (1, 3):
            @pl.when(relays(phase, c))
            def _():
                relay_copy(phase, c).wait_send()

        return carry

    lax.fori_loop(0, CHUNKS, finish, 0)


def write_out(fields, mass, temp, fields_out, mass_out, temp_out, sem):
    copies = [
        pltpu.make_async_copy(held, out, sem.at[k])
        for k, (held, out) in enumerate(((fields, fields_out), (mass, mass_out), (temp, temp_out)))
    ]
    for copy in copies:
        copy.start()
    for copy in copies:
        copy.wait()


def on_device(fields, velocity, noise, mixing_rate, parcel_cell, parcel_mass, parcel_temp):
    anywhere = pl.BlockSpec(memory_space=pl.ANY)
    in_vmem = pl.BlockSpec(memory_space=pltpu.VMEM)
    plane = (NY, NZ)
    block = (CX,) + plane
    dma = pltpu.SemaphoreType.DMA
    held = pl.pallas_call(
        kernel,
        out_shape=(
            pltpu.VMEM(fields.shape, F32),
            pltpu.VMEM(parcel_mass.shape, F32),
            pltpu.VMEM(parcel_temp.shape, F32),
        ),
        in_specs=[anywhere] * 7,
        out_specs=(in_vmem,) * 3,
        scratch_shapes=[
            pltpu.VMEM((2, S) + block, F32),
            pltpu.VMEM((4, 3, 2, S) + plane, F32),
            pltpu.VMEM(noise.shape, jnp.int32),
            pltpu.VMEM((3,) + block, F32),
            pltpu.VMEM(block, F32),
            pltpu.VMEM((2, 2, CX, 6) + plane, F32),
            pltpu.VMEM(block, F32),
            pltpu.VMEM((2, S) + block, F32),
            pltpu.VMEM((2, CHUNKS) + block, F32),
            pltpu.VMEM((2, CHUNKS) + block, F32),
            pltpu.VMEM((2, CHUNKS) + block, F32),
            pltpu.VMEM((2, S) + block, F32),
            pltpu.VMEM((2, ROWS, NZ), F32),
            pltpu.VMEM((GROUPS, 1, P_DEV), jnp.int32),
            pltpu.VMEM((GROUPS, 1, P_DEV), F32),
            pltpu.VMEM((GROUPS, 1, P_DEV), F32),
            dma((4,)),
            dma((3,)),
            dma((4, 2, CHUNKS)),
            dma((4, 3, CHUNKS)),
            dma((2, 3, CHUNKS)),
            dma((2, 3, CHUNKS)),
            dma((3, 3)),
            dma((3, 3)),
            dma((4, CHUNKS)),
        ],
        compiler_params=pltpu.CompilerParams(
            collective_id=0, has_side_effects=True, vmem_limit_bytes=57 << 20
        ),
    )(fields, velocity, noise, mixing_rate, parcel_cell, parcel_mass, parcel_temp)
    return pl.pallas_call(
        write_out,
        out_shape=tuple(jax.ShapeDtypeStruct(array.shape, F32) for array in held),
        in_specs=[anywhere] * 3,
        out_specs=(anywhere,) * 3,
        scratch_shapes=[dma((3,))],
        compiler_params=pltpu.CompilerParams(has_side_effects=True, vmem_limit_bytes=1 << 20),
    )(*held)


def solution(mesh):
    placed = (
        P("field", None, "space", None, None),
        P(None, "space", None, None),
        P(None, None, "field", None, "space", None, None),
        P("space", None, None),
        P("field", "space"),
        P("field", "space"),
        P("field", "space"),
    )
    return jax.shard_map(
        on_device,
        mesh=mesh,
        in_specs=placed,
        out_specs=(P("field", None, "space", None, None), P("field", "space"), P("field", "space")),
        check_vma=False,
    )
```
